512 devices in a mesh: bucket: 16 (over z_lo, x, core), edge: 32 (over z_hi, y).
Axes of the slice: x: 4, y: 8, z: 8 (z_hi: 4, z_lo: 2; z = z_hi * 2 + z_lo), core: 2. Of those that a mesh axis runs over, the one named last changes fastest.
Arguments:
- left_emb: float32 [131072, 400], P(('bucket', 'edge')), may hold values from -20 to 20
- right_emb: float32 [131072, 400], P(('bucket', 'edge')), may hold values from -20 to 20
- left_state: float32 [131072], P(('bucket', 'edge')), may hold values from 0.1 to 10
- right_state: float32 [131072], P(('bucket', 'edge')), may hold values from 0.1 to 10
- relations: float32 [1024, 400], replicated, may hold values from 0.1 to 1.9
- src_rows: int32 [16, 2, 8192], P('bucket', None, 'edge'), may hold values from 0 to 8191, as said below
- dst_rows: int32 [16, 2, 8192], P('bucket', None, 'edge'), may hold values from 0 to 8191, as said below
- rel_ids: int32 [16, 2, 8192], P('bucket', None, 'edge'), may hold values from 0 to 1023
- neg_rows: int32 [16, 2, 8192], P('bucket', None, 'edge'), may hold values from 0 to 8191, as said below
Outputs:
- left_next: float32 [131072, 400], P(('bucket', 'edge'))
- left_state_next: float32 [131072], P(('bucket', 'edge'))
- right_next: float32 [131072, 400], P(('bucket', 'edge'))
- right_state_next: float32 [131072], P(('bucket', 'edge'))
The draws below stay inside these ranges and needn't reach their ends.
Inputs may be any that keep to these rules, and one draw needn't show every extreme that they name: `src_rows`: of the 256 sources of one bucket, sub-round and index of edge, at most 12 lie in the rows held by any one index of edge; in each bucket and sub-round one index's rows receive exactly 12 from every index. `dst_rows`: likewise for the 256 destinations of one bucket, sub-round and index of edge. `neg_rows`: likewise for the 256 negatives of one bucket, sub-round and index of edge; a block's negatives may repeat rows and may equal its edges' destinations.
All inputs are finite; a program needn't handle non-finite values.
Results may differ from the reference program's by a relative error of at most 0.0037.
Values may be sent and summed in bfloat16 or wider, within the bound.
No kernel may reach another device: no remote copies, remote signals or barrier semaphores. Data moves between devices by JAX's collectives and lax.ppermute only.
A program may use at most 64 MiB of HBM per device.

```python
import math
import jax
import jax.numpy as jnp
from jax import lax

D = 400
CH = 256
NEG = 256
SUBS = 2
REL = 1024
R_DEV = 256
ROWS = 8192
BUCKETS = 16
EDGES = 8192
N_BUCKET = 16
N_EDGE = 32


def embed_rows(key, lower, upper):
    first = jax.random.fold_in(key, 0)
    fourth = jax.random.fold_in(key, 3)
    shape = (BUCKETS * ROWS, D)
    rough = jnp.clip(jax.random.normal(first, shape, jnp.float32), -6.0, 6.0)
    scale = jnp.exp(jax.random.uniform(fourth, (BUCKETS * ROWS, 1), jnp.float32, math.log(lower), math.log(upper)))
    return scale * rough


def draw_left_emb(key, part):
    key = jax.random.fold_in(key, 11)
    return embed_rows(key, 0.3, 3.0)


def draw_right_emb(key, part):
    key = jax.random.fold_in(key, 23)
    return embed_rows(key, 0.3, 3.0)


def routed_rows(key, count):
    holders = ROWS // R_DEV
    slot_cap = max(CH, NEG) // holders + 4
    slot_total = holders * slot_cap

    def one_list(list_key, full):
        first, second, third = jax.random.split(list_key, 3)
        score = jax.random.permutation(first, slot_total).astype(jnp.int32)
        owner_of = jnp.arange(slot_total, dtype=jnp.int32) // slot_cap
        score = score + jnp.where(owner_of == full, slot_total, 0).astype(jnp.int32)
        picked = jnp.argsort(-score, stable=True)[:count].astype(jnp.int32)
        picked = jax.random.permutation(second, picked)
        offset = jax.random.randint(third, (count,), 0, R_DEV, jnp.int32)
        return picked // slot_cap * R_DEV + offset

    def one_group(group_key):
        full = jax.random.randint(jax.random.fold_in(group_key, 0), (), 0, holders, jnp.int32)
        list_keys = jax.random.split(jax.random.fold_in(group_key, 1), holders)
        return jax.vmap(lambda sub_key: one_list(sub_key, full))(list_keys)
    group_keys = jax.random.split(key, BUCKETS * SUBS)
    lists = jax.vmap(one_group)(group_keys)
    return lists.reshape(BUCKETS, SUBS, holders * count).astype(jnp.int32)


def draw_src_rows(key, part):
    key = jax.random.fold_in(key, 31)
    return routed_rows(key, CH)


def draw_dst_rows(key, part):
    key = jax.random.fold_in(key, 37)
    return routed_rows(key, CH)


def draw_neg_rows(key, part):
    key = jax.random.fold_in(key, 41)
    return routed_rows(key, NEG)


def touch_ends(values, key, least, top_value):
    longest = values.shape.index(max(values.shape))
    spots = []
    for shift in (0, 1):
        where = [jax.random.randint(jax.random.fold_in(key, axis), (), 0, length) for axis, length in enumerate(values.shape)]
        where[longest] = (where[longest] + shift) % values.shape[longest]
        spots.append(tuple(where))
    return values.at[spots[0]].set(least).at[spots[1]].set(top_value)


def block_scale(key, shape, cuts, smallest, top_value):
    level = 1.0
    for position, parts in cuts:
        heights = jax.random.uniform(jax.random.fold_in(jax.random.fold_in(key, 6), position), (parts,), jnp.float32, smallest / len(cuts), top_value / len(cuts))
        level = level * jnp.repeat(jnp.exp(heights), shape[position] // parts).reshape((-1,) + (1,) * (len(shape) - 1 - position))
    return level


def setup_inputs(seed: int = 0) -> dict:
    keys = jax.random.split(jax.random.key(seed), 10)
    left_emb = draw_left_emb(jax.random.fold_in(keys[9], 71), 0)
    right_emb = draw_right_emb(jax.random.fold_in(keys[9], 71), 0)
    left_state = jnp.clip(jnp.exp(math.log(10.0) - 4.6051702 * jax.random.uniform(keys[2], (BUCKETS * ROWS,), jnp.float32) ** block_scale(keys[2], (BUCKETS * ROWS,), ((0, 512),), -0.2, 0.2)), 0.1, 10.0)
    right_state = jnp.clip(jnp.exp(math.log(10.0) - 4.6051702 * jax.random.uniform(keys[3], (BUCKETS * ROWS,), jnp.float32) ** block_scale(keys[3], (BUCKETS * ROWS,), ((0, 512),), -0.2, 0.2)), 0.1, 10.0)
    relations = jnp.clip(1.0 + 0.18 * jax.random.normal(keys[4], (REL, D), jnp.float32), 0.1, 1.9)
    src_rows = draw_src_rows(jax.random.fold_in(keys[9], 71), 0)
    dst_rows = draw_dst_rows(jax.random.fold_in(keys[9], 71), 0)
    rel_ids = touch_ends(jax.random.randint(keys[7], (BUCKETS, SUBS, EDGES), 0, REL), jax.random.fold_in(keys[7], 1), 0, REL - 1).astype(jnp.int32)
    neg_rows = draw_neg_rows(jax.random.fold_in(keys[9], 71), 0)
    return {"left_emb": left_emb, "right_emb": right_emb, "left_state": left_state, "right_state": right_state, "relations": relations, "src_rows": src_rows, "dst_rows": dst_rows, "rel_ids": rel_ids, "neg_rows": neg_rows}


sharp = 40.0
rate = 0.5
tiny = 1e-06
guard = 1e-10

def unit(vectors):
    length = jnp.sqrt(lax.optimization_barrier(jnp.sum(vectors * vectors, axis=-1, keepdims=True)) + tiny)
    return (vectors / length, length)

def unit_back(grad, direction, length):
    return (grad - direction * lax.optimization_barrier(jnp.sum(direction * grad, axis=-1, keepdims=True))) / length

def contract(first, second, dims):
    return lax.dot_general(first, second, (dims, ((), ())), preferred_element_type=jnp.float32)

def block_grads(left_copy, right_copy, relations, sources, targets, kinds, noises):
    scale = relations[kinds]
    query, query_len = unit(left_copy[sources].astype(jnp.float32) * scale)
    target, target_len = unit(right_copy[targets].astype(jnp.float32))
    noise, noise_len = unit(right_copy[noises].astype(jnp.float32))
    query_half = query.astype(jnp.bfloat16)
    noise_half = noise.astype(jnp.bfloat16)
    positive = sharp * lax.optimization_barrier(jnp.sum(query * target, axis=1))
    scores = sharp * contract(query_half, noise_half, ((1,), (1,)))
    raised = jnp.exp(positive)
    spread = jnp.exp(scores)
    total = raised + lax.optimization_barrier(jnp.sum(spread, axis=1))
    miss = raised / total - 1.0
    weights = (spread / total[:, None]).astype(jnp.bfloat16)
    query_grad = sharp * (miss[:, None] * target + contract(weights, noise_half, ((1,), (0,))))
    target_grad = sharp * miss[:, None] * query
    noise_grad = sharp * contract(weights, query_half, ((0,), (0,)))
    return (unit_back(query_grad, query, query_len) * scale, unit_back(target_grad, target, target_len), unit_back(noise_grad, noise, noise_len))

def adagrad(matrix, state, grad):
    state = state + lax.optimization_barrier(jnp.mean(grad * grad, axis=1))
    return (matrix - rate * grad / (jnp.sqrt(state)[:, None] + guard), state)

def reference(left_emb, right_emb, left_state, right_state, relations, src_rows, dst_rows, rel_ids, neg_rows):
    left = left_emb.reshape(N_BUCKET, ROWS, D)
    right = right_emb.reshape(N_BUCKET, ROWS, D)
    left_acc = left_state.reshape(N_BUCKET, ROWS)
    right_acc = right_state.reshape(N_BUCKET, ROWS)
    for step in range(SUBS):

        def bucket(items):
            left_part, right_part, left_hist, right_hist, sources, targets, kinds, noises = items
            left_copy = left_part.astype(jnp.bfloat16)
            right_copy = right_part.astype(jnp.bfloat16)

            def block(carry, pieces):
                left_grad, right_grad = carry
                source, target, kind, noise = pieces
                grads = block_grads(left_copy, right_copy, relations, source, target, kind, noise)
                left_grad = left_grad + jax.ops.segment_sum(grads[0], source, num_segments=ROWS)
                right_grad = right_grad + jax.ops.segment_sum(grads[1], target, num_segments=ROWS)
                right_grad = right_grad + jax.ops.segment_sum(grads[2], noise, num_segments=ROWS)
                return ((left_grad, right_grad), None)
            zeros = jnp.zeros((ROWS, D), jnp.float32)
            (left_grad, right_grad), unused = lax.scan(block, (zeros, zeros), (sources.reshape(N_EDGE, CH), targets.reshape(N_EDGE, CH), kinds.reshape(N_EDGE, CH), noises.reshape(N_EDGE, NEG)))
            left_new, left_hist = adagrad(left_part, left_hist, left_grad)
            right_new, right_hist = adagrad(right_part, right_hist, right_grad)
            return (left_new, right_new, left_hist, right_hist)
        left, right, left_acc, right_acc = lax.map(bucket, (left, right, left_acc, right_acc, src_rows[:, step], dst_rows[:, step], rel_ids[:, step], neg_rows[:, step]))
    right = jnp.roll(right, 1, axis=0)
    right_acc = jnp.roll(right_acc, 1, axis=0)
    return (left.reshape(N_BUCKET * ROWS, D), left_acc.reshape(N_BUCKET * ROWS), right.reshape(N_BUCKET * ROWS, D), right_acc.reshape(N_BUCKET * ROWS))
```

```python
import jax
import jax.numpy as jnp
from jax import lax
from jax.experimental import pallas as pl
from jax.experimental.pallas import tpu as pltpu
from jax.sharding import PartitionSpec as P

SUBS = 2
D = 400
K = 256
HOLD = 32
CAP = 12
LANE = 128
WIDE = 512
TAIL = 16
REST = 3 * LANE
SLOT_A = 32
SLOT_B = 8
ROW_A = HOLD * SLOT_A
ROWS_J = HOLD * (SLOT_A + SLOT_B)
BLOCK = 3 * (SLOT_A + SLOT_B)
STEP = 64

sharp = 40.0
rate = 0.5
tiny = 1e-06
guard = 1e-10

f32 = jnp.float32
bf16 = jnp.bfloat16
i32 = jnp.int32


def iota(shape, dim):
    return lax.broadcasted_iota(i32, shape, dim)


def mm(first, second):
    return lax.dot_general(first, second, (((1,), (0,)), ((), ())), preferred_element_type=f32)


def mm_nt(first, second):
    return lax.dot_general(first, second, (((1,), (1,)), ((), ())), preferred_element_type=f32)


def as_half(mask):
    return mask.astype(f32).astype(bf16)


def plan_kernel(src_ref, dst_ref, neg_ref, want_ref, place_ref):
    refs = (src_ref, dst_ref, neg_ref)
    lists = [refs[kind][step : step + 1, :] for step in range(SUBS) for kind in range(3)]
    holder = iota((HOLD, K), 0)
    hits = [(holder == (row >> 8)).astype(f32) for row in lists]
    upto = as_half(iota((K, K), 0) <= iota((K, K), 1))
    counts = mm(jnp.concatenate(hits, axis=0).astype(bf16), upto)
    want = jnp.zeros((HOLD, LANE), f32)
    slots = iota((LANE, K), 0)
    places = []
    for number, row in enumerate(lists):
        step, kind = divmod(number, 3)
        hit = hits[number]
        count = counts[number * HOLD : (number + 1) * HOLD, :]
        order = jnp.sum(hit * count, axis=0, keepdims=True).astype(i32) - 1
        slot = order + kind * CAP
        owner = row >> 8
        local = (row & 255).astype(f32)
        chosen = as_half(slots == slot + step * STEP)
        want = want + mm_nt((hit * local).astype(bf16), chosen)
        places.append(
            jnp.where(slot < SLOT_A, owner * SLOT_A + slot, ROW_A + owner * SLOT_B + slot - SLOT_A)
        )
    places.append(jnp.zeros((2, K), i32))
    place_ref[...] = jnp.concatenate(places, axis=0)
    slot = iota((HOLD, LANE), 1) & (STEP - 1)
    base = jnp.where(slot < CAP, 0, jnp.where(slot < 3 * CAP, K, 4 * K))
    want_ref[:, 0, :] = want.astype(i32) + base


def edge_kernel(place_ref, *out_refs):
    place = place_ref[...].astype(f32)
    tall = jnp.concatenate([place, jnp.zeros((LANE - 8, K), f32)], axis=0)
    columns = jnp.transpose(tall).astype(i32)
    for step in range(SUBS):
        to_slot, to_edge = out_refs[2 * step], out_refs[2 * step + 1]
        for kind in range(3):
            number = step * 3 + kind
            to_slot[:, kind * K : (kind + 1) * K] = as_half(
                iota((ROWS_J, K), 0) == place_ref[number : number + 1, :]
            )
            to_edge[kind * K : (kind + 1) * K, :] = as_half(
                iota((K, ROWS_J), 1) == columns[:, number : number + 1]
            )


def asked(got_ref, step):
    got = got_ref[:, 0, :].astype(f32)
    square = jnp.concatenate([got, jnp.zeros((LANE - HOLD, LANE), f32)], axis=0)
    turned = jnp.transpose(square).astype(i32)
    low = step * STEP
    parts = []
    for start, size in ((low, SLOT_A), (low + SLOT_A, SLOT_B)):
        for holder in range(HOLD):
            column = turned[start : start + size, holder : holder + 1]
            parts.append((iota((size, 2 * K), 1) == column).astype(f32))
    return jnp.concatenate(parts, axis=0)


def held_kernel(got_ref, sum_first_ref, serve_ref, sum_second_ref):
    sum_first_ref[...] = jnp.transpose(asked(got_ref, 0)).astype(bf16)
    second = asked(got_ref, 1)
    serve_ref[...] = second.astype(bf16)
    sum_second_ref[...] = jnp.transpose(second).astype(bf16)


def group_mask(shape):
    return (iota(shape, len(shape) - 1) >> 4) == iota(shape, len(shape) - 2)


def pack(values, out_ref):
    keep = group_mask((HOLD, SLOT_B, LANE))
    sub = iota((HOLD, SLOT_B, LANE), 1)
    firsts = values[:ROW_A].reshape(HOLD, SLOT_A, WIDE)
    lasts = values[ROW_A:].reshape(HOLD, SLOT_B, WIDE)
    ends = [lasts[:, :, c * LANE : (c + 1) * LANE] for c in range(3)]
    for c in range(3):
        out_ref[:, c * SLOT_A : (c + 1) * SLOT_A, :] = firsts[
            :, :, c * LANE : (c + 1) * LANE
        ].astype(bf16)
    for m in range(4):
        piece = firsts[:, m * 8 : (m + 1) * 8, REST:]
        row = jnp.sum(jnp.where(keep, piece, 0.0), axis=1, keepdims=True)
        ends[0] = jnp.where(sub == 4 + m, row, ends[0])
    row = jnp.sum(jnp.where(keep, lasts[:, :, REST:], 0.0), axis=1, keepdims=True)
    ends[1] = jnp.where(sub == 4, row, ends[1])
    out_ref[:, 3 * SLOT_A :, :] = jnp.concatenate(ends, axis=1).astype(bf16)


def unpack(in_ref):
    keep = group_mask((HOLD, SLOT_B, LANE))
    ends = in_ref[:, 3 * SLOT_A :, :].astype(f32)
    tails = []
    for m in range(5):
        at = 4 + m if m < 4 else 12
        row = ends[:, at : at + 1, :]
        tails.append(jnp.where(keep, row, 0.0))
    chunks = []
    for c in range(3):
        first = in_ref[:, c * SLOT_A : (c + 1) * SLOT_A, :].reshape(ROW_A, LANE)
        last = ends[:, c * 8 : (c + 1) * 8, :].reshape(HOLD * SLOT_B, LANE).astype(bf16)
        chunks.append(jnp.concatenate([first, last], axis=0))
    first = jnp.concatenate(tails[:4], axis=1).reshape(ROW_A, LANE).astype(bf16)
    last = tails[4].reshape(HOLD * SLOT_B, LANE).astype(bf16)
    chunks.append(jnp.concatenate([first, last], axis=0))
    return jnp.concatenate(chunks, axis=1)


def fold(values):
    tail = values[:, REST:]
    for shift in (64, 32, 16):
        tail = tail + pltpu.roll(tail, shift, 1)
    return tail


def once(tail):
    return jnp.where(iota(tail.shape, 1) < TAIL, tail, 0.0)


def spread_tail(values):
    tail = values[:, REST:]
    for shift in (16, 32, 64):
        tail = tail + pltpu.roll(tail, shift, 1)
    return jnp.concatenate([values[:, :REST], tail], axis=1)


def serve(chosen, left, right, out_ref):
    both = jnp.concatenate([left, right], axis=1)
    table = jnp.concatenate([both[:REST]] + [both[REST:]] * 8, axis=0).astype(bf16)
    pack(mm_nt(chosen, table), out_ref)


def serve_kernel(left_ref, right_ref, got_ref, out_ref):
    serve(asked(got_ref, 0).astype(bf16), left_ref[...], right_ref[...], out_ref)


def unit(vectors):
    length = jnp.sqrt(jnp.sum(vectors * vectors, axis=-1, keepdims=True) + tiny)
    return vectors / length, length


def unit_back(grad, direction, length):
    return (grad - direction * jnp.sum(direction * grad, axis=-1, keepdims=True)) / length


def grad_kernel(in_ref, to_edge_ref, to_slot_ref, scale_ref, out_ref):
    rows = unpack(in_ref)

    def picked(kind):
        values = mm(to_edge_ref[kind * K : (kind + 1) * K, :], rows)
        return jnp.concatenate([values[:, :REST], once(fold(values))], axis=1)

    scale = scale_ref[...]
    query, query_len = unit(picked(0) * scale)
    noise, noise_len = unit(picked(2))
    query_half = query.astype(bf16)
    noise_half = noise.astype(bf16)
    target, target_len = unit(picked(1))
    positive = sharp * jnp.sum(query * target, axis=1, keepdims=True)
    scores = sharp * mm_nt(query_half, noise_half)
    raised = jnp.exp(positive)
    spread = jnp.exp(scores)
    total = raised + jnp.sum(spread, axis=1, keepdims=True)
    miss = raised / total - 1.0
    weights = spread / total
    query_grad = sharp * (miss * target + mm(weights.astype(bf16), noise_half))
    target_grad = sharp * miss * query
    noise_grad = sharp * mm(jnp.transpose(weights).astype(bf16), query_half)
    grads = [
        unit_back(query_grad, query, query_len) * scale,
        unit_back(target_grad, target, target_len),
        unit_back(noise_grad, noise, noise_len),
    ]
    together = jnp.concatenate([spread_tail(grad).astype(bf16) for grad in grads], axis=0)
    pack(mm(to_slot_ref[...], together), out_ref)


def adagrad(matrix, state, grad):
    state = state + jnp.sum(grad * grad, axis=0, keepdims=True) / D
    return matrix - rate * grad / (jnp.sqrt(state) + guard), state


def update(in_ref, to_row_ref, left_ref, right_ref, left_state_ref, right_state_ref):
    values = mm(to_row_ref[...], unpack(in_ref))
    values = jnp.concatenate([values[:, :REST], fold(values)], axis=1)
    turned = jnp.transpose(values)[:D]
    left, left_state = adagrad(left_ref[...], left_state_ref[...], turned[:, :K])
    right, right_state = adagrad(right_ref[...], right_state_ref[...], turned[:, K:])
    return left, left_state, right, right_state


def next_kernel(
    in_ref, to_row_ref, left_ref, right_ref, left_state_ref, right_state_ref, serve_ref,
    out_ref, left_out, left_state_out, right_out, right_state_out,
):
    left, left_state, right, right_state = update(
        in_ref, to_row_ref, left_ref, right_ref, left_state_ref, right_state_ref
    )
    left_out[...], left_state_out[...] = left, left_state
    right_out[...], right_state_out[...] = right, right_state
    serve(serve_ref[...], left, right, out_ref)


def last_kernel(
    in_ref, to_row_ref, left_ref, right_ref, left_state_ref, right_state_ref,
    left_out, left_state_out, right_out, right_state_out,
):
    left, left_state, right, right_state = update(
        in_ref, to_row_ref, left_ref, right_ref, left_state_ref, right_state_ref
    )
    left_out[...], left_state_out[...] = left, left_state
    right_out[...], right_state_out[...] = right, right_state


def call(kernel, outs, *args, flops=0):
    size = sum(x.size * x.dtype.itemsize for x in list(args) + list(outs))
    spec = pl.BlockSpec(memory_space=pltpu.VMEM)
    return pl.pallas_call(
        kernel,
        out_shape=tuple(outs),
        in_specs=[spec] * len(args),
        out_specs=tuple([spec] * len(outs)),
        compiler_params=pltpu.CompilerParams(vmem_limit_bytes=40 * 1024 * 1024),
        cost_estimate=pl.CostEstimate(flops=flops, bytes_accessed=size, transcendentals=0),
    )(*args)


def shape(dims, dtype):
    return jax.ShapeDtypeStruct(dims, dtype)


def exchange(blocks):
    return lax.all_to_all(blocks, "edge", split_axis=0, concat_axis=0, tiled=True)


def shifted(value, axis, steps):
    count = lax.axis_size(axis)
    pairs = [(source, (source + steps) % count) for source in range(count)]
    return lax.ppermute(value, axis, pairs)


BLOCKS = shape((HOLD, BLOCK, LANE), bf16)
TABLE = shape((D, K), f32)
STATE = shape((1, K), f32)


def on_device(
    left_emb, right_emb, left_state, right_state, relations, src_rows, dst_rows, rel_ids, neg_rows
):
    left, right = left_emb.T, right_emb.T
    left_hist, right_hist = left_state.reshape(1, K), right_state.reshape(1, K)
    want, place = call(
        plan_kernel,
        [shape((HOLD, 1, LANE), i32), shape((8, K), i32)],
        src_rows[0], dst_rows[0], neg_rows[0],
    )
    got = exchange(want)
    to_slot_0, to_edge_0, to_slot_1, to_edge_1 = call(
        edge_kernel,
        [shape((ROWS_J, 3 * K), bf16), shape((3 * K, ROWS_J), bf16)] * 2,
        place,
    )
    scales = jnp.pad(relations[rel_ids[0].reshape(-1)], ((0, 0), (0, WIDE - D)))
    (blocks,) = call(serve_kernel, [BLOCKS], left, right, got)
    blocks = exchange(blocks)
    sum_first, serve_second, sum_second = call(
        held_kernel,
        [
            shape((2 * K, ROWS_J), bf16),
            shape((ROWS_J, 2 * K), bf16),
            shape((2 * K, ROWS_J), bf16),
        ],
        got,
    )
    (blocks,) = call(grad_kernel, [BLOCKS], blocks, to_edge_0, to_slot_0, scales[:K])
    blocks = exchange(blocks)
    blocks, left, left_hist, right, right_hist = call(
        next_kernel,
        [BLOCKS, TABLE, STATE, TABLE, STATE],
        blocks, sum_first, left, right, left_hist, right_hist, serve_second,
    )
    blocks = exchange(blocks)
    (blocks,) = call(grad_kernel, [BLOCKS], blocks, to_edge_1, to_slot_1, scales[K:])
    blocks = exchange(blocks)
    left, left_hist, right, right_hist = call(
        last_kernel,
        [TABLE, STATE, TABLE, STATE],
        blocks, sum_second, left, right, left_hist, right_hist,
    )
    right, right_hist = shifted((right, right_hist), "bucket", 1)
    return (left.T, left_hist.reshape(K), right.T, right_hist.reshape(K))


def solution(mesh):
    return jax.shard_map(
        on_device,
        mesh=mesh,
        in_specs=(
            P(("bucket", "edge"), None),
            P(("bucket", "edge"), None),
            P(("bucket", "edge")),
            P(("bucket", "edge")),
            P(),
            P("bucket", None, "edge"),
            P("bucket", None, "edge"),
            P("bucket", None, "edge"),
            P("bucket", None, "edge"),
        ),
        out_specs=(
            P(("bucket", "edge"), None),
            P(("bucket", "edge")),
            P(("bucket", "edge"), None),
            P(("bucket", "edge")),
        ),
        check_vma=False,
    )
```

```python
import functools

import jax
import jax.numpy as jnp
from jax import lax
from jax.experimental import pallas as pl
from jax.experimental.pallas import tpu as pltpu
from jax.sharding import PartitionSpec as P

SUBS = 2
D = 400
K = 256
HOLD = 32
CAP = 12
LANE = 128
WIDE = 512
TAIL = 16
REST = 3 * LANE
GROUP = 8
GROUPS = 5
PARTS = 6
GROUP_OF = (0, 1, 2, 3, 3, 4)
USED = 36
BLOCK = 3 * GROUPS * GROUP
MIB = 1024 * 1024
STEP = 64

sharp = 40.0
rate = 0.5
tiny = 1e-06
guard = 1e-10

f32 = jnp.float32
bf16 = jnp.bfloat16
i32 = jnp.int32


def iota(shape, dim):
    return lax.broadcasted_iota(i32, shape, dim)


def mm(first, second):
    return lax.dot_general(first, second, (((1,), (0,)), ((), ())), preferred_element_type=f32)


def mm_nt(first, second):
    return lax.dot_general(first, second, (((1,), (1,)), ((), ())), preferred_element_type=f32)


def as_half(mask):
    return mask.astype(f32).astype(bf16)


def load(pairs, sems):
    copies = [
        pltpu.make_async_copy(source, target, sems.at[number])
        for number, (source, target) in enumerate(pairs)
    ]
    for copy in copies:
        copy.start()
    return copies


def plan_kernel(src_far, dst_far, neg_far, want_ref, place_ref, src_ref, dst_ref, neg_ref, sems):
    refs = (src_ref, dst_ref, neg_ref)
    loads = load(zip((src_far, dst_far, neg_far), refs), sems)
    for copy in loads:
        copy.wait()
    lists = [refs[kind][step : step + 1, :] for step in range(SUBS) for kind in range(3)]
    holder = iota((HOLD, K), 0)
    hits = [(holder == (row >> 8)).astype(f32) for row in lists]
    upto = as_half(iota((K, K), 0) <= iota((K, K), 1))
    counts = mm(jnp.concatenate(hits, axis=0).astype(bf16), upto)
    want = jnp.zeros((HOLD, LANE), f32)
    slots = iota((LANE, K), 0)
    firsts, lasts = [], []
    for number, row in enumerate(lists):
        step, kind = divmod(number, 3)
        hit = hits[number]
        count = counts[number * HOLD : (number + 1) * HOLD, :]
        order = jnp.sum(hit * count, axis=0, keepdims=True).astype(i32) - 1
        early = order < GROUP
        late = order - GROUP + (4 if kind == 1 else 0)
        slot = jnp.where(early, kind * GROUP + order, GROUP_OF[3 + kind] * GROUP + late)
        owner = row >> 8
        local = (row & 255).astype(f32)
        chosen = as_half(slots == slot + step * STEP)
        want = want + mm_nt((hit * local).astype(bf16), chosen)
        firsts.append(jnp.where(early, owner * GROUP + order, -1))
        lasts.append(jnp.where(early, -1, owner * GROUP + late))
    places = firsts[:3] + lasts[:3] + firsts[3:] + lasts[3:] + [jnp.full((4, K), -1, i32)]
    place_ref[...] = jnp.concatenate(places, axis=0)
    slot = iota((HOLD, LANE), 1) & (STEP - 1)
    want_ref[:, 0, :] = want.astype(i32) + jnp.where(slot < USED, 0, 2 * K)


def part(number):
    return slice(number * K, (number + 1) * K)


def asked(got_ref, step):
    got = got_ref[:, 0, :].astype(f32)
    square = jnp.concatenate([got, jnp.zeros((LANE - HOLD, LANE), f32)], axis=0)
    turned = jnp.transpose(square).astype(i32)
    groups = []
    for group in range(GROUPS):
        start = step * STEP + group * GROUP
        rows = [
            (iota((GROUP, K), 1) == turned[start : start + GROUP, holder : holder + 1]).astype(f32)
            for holder in range(HOLD)
        ]
        groups.append(jnp.concatenate(rows, axis=0))
    half = (iota((K, K), 0) & (GROUP - 1)) < 4
    shared = groups[3]
    return groups[:3] + [jnp.where(half, shared, 0.0), jnp.where(half, 0.0, shared), groups[4]]


def held_kernel(step, got_ref, token_ref, sum_ref):
    del token_ref
    for number, rows in enumerate(asked(got_ref, step)):
        sum_ref[part(number), :] = jnp.transpose(rows).astype(bf16)


def group_mask(shape):
    return (iota(shape, len(shape) - 1) >> 4) == iota(shape, len(shape) - 2)


def pack(values, out_ref):
    keep = group_mask((HOLD, GROUP, LANE))
    sub = iota((HOLD, GROUP, LANE), 1)
    values = [value.reshape(HOLD, GROUP, WIDE) for value in values]
    pieces = [[value[:, :, c * LANE : (c + 1) * LANE] for value in values] for c in range(3)]
    for group, value in enumerate(values):
        row = jnp.sum(jnp.where(keep, value[:, :, REST:], 0.0), axis=1, keepdims=True)
        c, at = divmod(group, 4)
        pieces[c][4] = jnp.where(sub == 4 + at, row, pieces[c][4])
    out_ref[...] = jnp.concatenate(pieces[0] + pieces[1] + pieces[2], axis=1).astype(bf16)


def unpack(in_ref):
    keep = group_mask((HOLD, GROUP, LANE))
    rows = in_ref[...].astype(f32)
    groups = []
    for group in range(GROUPS):
        chunks = []
        for c in range(3):
            start = (c * GROUPS + group) * GROUP
            chunks.append(rows[:, start : start + GROUP, :])
        c, at = divmod(group, 4)
        start = (c * GROUPS + 4) * GROUP + 4 + at
        chunks.append(jnp.where(keep, rows[:, start : start + 1, :], 0.0))
        groups.append(
            jnp.concatenate([x.reshape(K, LANE) for x in chunks], axis=1).astype(bf16)
        )
    return groups


def fold(values):
    tail = values[:, REST:]
    for shift in (64, 32, 16):
        tail = tail + pltpu.roll(tail, shift, 1)
    return tail


def once(tail):
    return jnp.where(iota(tail.shape, 1) < TAIL, tail, 0.0)


def spread_tail(values):
    tail = values[:, REST:]
    for shift in (16, 32, 64):
        tail = tail + pltpu.roll(tail, shift, 1)
    return jnp.concatenate([values[:, :REST], tail], axis=1)


def table_of(values):
    return jnp.concatenate([values[:REST]] + [values[REST:]] * 8, axis=0).astype(bf16)


def table_kernel(left_ref, right_ref, place_ref, out_ref, column_ref):
    place = place_ref[...].astype(f32)
    tall = jnp.concatenate([place, jnp.zeros((LANE - 16, K), f32)], axis=0)
    column_ref[...] = jnp.transpose(tall).astype(i32)
    out_ref[:, :K] = table_of(left_ref[...])
    out_ref[:, K:] = table_of(right_ref[...])


def serve(parts, left, right, out_ref):
    tables = (left, right, right, left, right, right)
    values = [mm_nt(rows, table) for rows, table in zip(parts, tables)]
    pack(values[:3] + [values[3] + values[4], values[5]], out_ref)


def serve_kernel(table_ref, got_ref, out_ref, token_ref):
    token_ref[...] = jnp.zeros_like(token_ref)
    parts = [rows.astype(bf16) for rows in asked(got_ref, 0)]
    serve(parts, table_ref[:, :K], table_ref[:, K:], out_ref)


def unit(vectors):
    inverse = 1.0 / jnp.sqrt(jnp.sum(vectors * vectors, axis=-1, keepdims=True) + tiny)
    return vectors * inverse, inverse


def unit_back(grad, direction, inverse):
    return (grad - direction * jnp.sum(direction * grad, axis=-1, keepdims=True)) * inverse


def grad_kernel(step, in_ref, column_ref, place_ref, scale_ref, *refs):
    out_ref = refs[-1]
    rows = unpack(in_ref)

    def picked_part(number):
        at = step * PARTS + number
        to_edge = as_half(iota((K, K), 1) == column_ref[:, at : at + 1])
        return mm(to_edge, rows[GROUP_OF[number]])

    def picked(kind):
        values = picked_part(kind) + picked_part(3 + kind)
        return jnp.concatenate([values[:, :REST], once(fold(values))], axis=1)

    scale = scale_ref[...]
    query, query_inv = unit(picked(0) * scale)
    noise, noise_inv = unit(picked(2))
    query_half = query.astype(bf16)
    noise_half = noise.astype(bf16)
    target, target_inv = unit(picked(1))
    positive = sharp * jnp.sum(query * target, axis=1, keepdims=True)
    scores = sharp * mm_nt(query_half, noise_half)
    raised = jnp.exp(positive)
    spread = jnp.exp(scores)
    total = raised + jnp.sum(spread, axis=1, keepdims=True)
    share = 1.0 / total
    miss = raised * share - 1.0
    weights = spread * share
    query_grad = sharp * (miss * target + mm(weights.astype(bf16), noise_half))
    target_grad = sharp * miss * query
    noise_grad = sharp * mm(jnp.transpose(weights).astype(bf16), query_half)
    grads = [
        unit_back(query_grad, query, query_inv) * scale,
        unit_back(target_grad, target, target_inv),
        unit_back(noise_grad, noise, noise_inv),
    ]
    grads = [spread_tail(grad).astype(bf16) for grad in grads]
    values = []
    for number in range(PARTS):
        at = step * PARTS + number
        to_slot = as_half(iota((K, K), 0) == place_ref[at : at + 1, :])
        values.append(mm(to_slot, grads[number % 3]))
    pack(values[:3] + [values[3] + values[4], values[5]], out_ref)


def adagrad(matrix, state, grad):
    state = state + jnp.sum(grad * grad, axis=0, keepdims=True) / D
    return matrix - grad * (rate / (jnp.sqrt(state) + guard)), state


def row_grads(rows, to_row_ref, numbers):
    values = sum(mm(to_row_ref[part(number), :], rows[GROUP_OF[number]]) for number in numbers)
    values = jnp.concatenate([values[:, :REST], fold(values)], axis=1)
    return jnp.transpose(values)[:D]


LEFT = (0, 3)
RIGHT = (1, 2, 4, 5)


def update(in_ref, to_row_ref, left_ref, right_ref, left_state_ref, right_state_ref):
    rows = unpack(in_ref)
    left = adagrad(left_ref[...], left_state_ref[...], row_grads(rows, to_row_ref, LEFT))
    right = adagrad(right_ref[...], right_state_ref[...], row_grads(rows, to_row_ref, RIGHT))
    return left, right


def next_kernel(
    in_ref, to_row_ref, left_ref, right_ref, left_state_ref, right_state_ref, got_ref,
    out_ref, token_ref,
):
    left, right = update(
        in_ref, to_row_ref, left_ref, right_ref, left_state_ref, right_state_ref
    )
    token_ref[...] = left[0][:8, :LANE]
    parts = [rows.astype(bf16) for rows in asked(got_ref, 1)]
    serve(parts, table_of(left[0]), table_of(right[0]), out_ref)


def update_kernel(
    in_ref, to_row_ref, left_ref, right_ref, left_state_ref, right_state_ref, token_ref,
    left_out, left_state_out, right_out, right_state_out,
):
    del token_ref
    left, right = update(
        in_ref, to_row_ref, left_ref, right_ref, left_state_ref, right_state_ref
    )
    left_out[...], left_state_out[...] = left
    right_out[...], right_state_out[...] = right


def right_last_kernel(in_ref, to_row_ref, right_ref, right_state_ref, joined_ref):
    grads = row_grads(unpack(in_ref), to_row_ref, RIGHT)
    right, state = adagrad(right_ref[...], right_state_ref[...], grads)
    joined_ref[...] = jnp.concatenate([right, jnp.broadcast_to(state, (8, K))], axis=0)


def left_last_kernel(in_ref, to_row_ref, left_ref, left_state_ref, left_out, left_state_out):
    grads = row_grads(unpack(in_ref), to_row_ref, LEFT)
    left_out[...], left_state_out[...] = adagrad(left_ref[...], left_state_ref[...], grads)


def call(kernel, outs, *args, far=(), scratch=(), copies=0, grant=16):
    size = sum(x.size * x.dtype.itemsize for x in list(args) + list(outs))
    held = pl.BlockSpec(memory_space=pltpu.VMEM)
    away = pl.BlockSpec(memory_space=pltpu.HBM)
    scratch = [pltpu.VMEM(x.shape, x.dtype) for x in scratch]
    if copies:
        scratch.append(pltpu.SemaphoreType.DMA((copies,)))
    return pl.pallas_call(
        kernel,
        out_shape=tuple(outs),
        in_specs=[away if number in far else held for number in range(len(args))],
        out_specs=tuple([held] * len(outs)),
        scratch_shapes=scratch,
        compiler_params=pltpu.CompilerParams(vmem_limit_bytes=grant * MIB),
        cost_estimate=pl.CostEstimate(flops=0, bytes_accessed=size, transcendentals=0),
    )(*args)


def shape(dims, dtype):
    return jax.ShapeDtypeStruct(dims, dtype)


def exchange(blocks):
    return lax.all_to_all(blocks, "edge", split_axis=0, concat_axis=0, tiled=True)


def exchange_in_turn(want):
    even = lax.axis_index("bucket") % 2 == 0
    count = lax.axis_size("bucket")
    first = lax.cond(even, exchange, jnp.zeros_like, want)
    signal = lax.ppermute(first[0], "bucket", [(b, b + 1) for b in range(0, count - 1, 2)])
    want = jnp.where(signal[0, 0] < 0, 0, want)
    return lax.cond(even, lambda one, two: one, lambda one, two: exchange(two), first, want)


def shifted(value, axis, steps):
    count = lax.axis_size(axis)
    pairs = [(source, (source + steps) % count) for source in range(count)]
    return lax.ppermute(value, axis, pairs)


BLOCKS = shape((HOLD, BLOCK, LANE), bf16)
TABLE = shape((D, K), f32)
STATE = shape((1, K), f32)
LIST = shape((SUBS, K), i32)
HOT = shape((PARTS * K, K), bf16)
TOKEN = shape((8, LANE), f32)


def holds_of(step, got, token):
    return call(functools.partial(held_kernel, step), [HOT], got, token)[0]


def grads_of(step, blocks, columns, place, scales, *tokens):
    return call(
        functools.partial(grad_kernel, step), [BLOCKS],
        blocks, columns, place, scales[step * K : (step + 1) * K], *tokens,
    )[0]


def on_device(
    left_emb, right_emb, left_state, right_state, relations, src_rows, dst_rows, rel_ids, neg_rows
):
    left, right = left_emb.T, right_emb.T
    left_hist, right_hist = left_state.reshape(1, K), right_state.reshape(1, K)
    want, place = call(
        plan_kernel, [shape((HOLD, 1, LANE), i32), shape((16, K), i32)],
        src_rows[0], dst_rows[0], neg_rows[0],
        far=(0, 1, 2), scratch=(LIST, LIST, LIST), copies=3, grant=62,
    )
    got = exchange_in_turn(want)
    scales = jnp.pad(relations[rel_ids[0].reshape(-1)], ((0, 0), (0, WIDE - D)))
    table, columns = call(
        table_kernel, [shape((WIDE, 2 * K), bf16), shape((K, LANE), i32)], left, right, place
    )
    blocks, token = call(serve_kernel, [BLOCKS, TOKEN], table, got)
    blocks = exchange(blocks)
    to_row = holds_of(0, got, token)
    blocks = grads_of(0, blocks, columns, place, scales, to_row)
    blocks = exchange(blocks)
    held = (blocks, to_row, left, right, left_hist, right_hist)
    blocks, token = call(next_kernel, [BLOCKS, TOKEN], *held, got)
    blocks = exchange(blocks)
    left, left_hist, right, right_hist = call(
        update_kernel, [TABLE, STATE, TABLE, STATE], *held, token
    )
    to_row = holds_of(1, got, left_hist)
    blocks = grads_of(1, blocks, columns, place, scales, to_row)
    blocks = exchange(blocks)
    (joined,) = call(
        right_last_kernel, [shape((D + 8, K), f32)], blocks, to_row, right, right_hist
    )
    joined = shifted(joined, "bucket", 1)
    left, left_hist = call(left_last_kernel, [TABLE, STATE], blocks, to_row, left, left_hist)
    return (left.T, left_hist.reshape(K), joined[:D].T, joined[D])


def solution(mesh):
    return jax.shard_map(
        on_device,
        mesh=mesh,
        in_specs=(
            P(("bucket", "edge"), None),
            P(("bucket", "edge"), None),
            P(("bucket", "edge")),
            P(("bucket", "edge")),
            P(),
            P("bucket", None, "edge"),
            P("bucket", None, "edge"),
            P("bucket", None, "edge"),
            P("bucket", None, "edge"),
        ),
        out_specs=(
            P(("bucket", "edge"), None),
            P(("bucket", "edge")),
            P(("bucket", "edge"), None),
            P(("bucket", "edge")),
        ),
        check_vma=False,
    )
```

```python
import functools

import jax
import jax.numpy as jnp
from jax import lax
from jax.experimental import pallas as pl
from jax.experimental.pallas import tpu as pltpu
from jax.sharding import PartitionSpec as P

SUBS = 2
D = 400
K = 256
HOLD = 32
CAP = 12
LANE = 128
WIDE = 512
TAIL = 16
REST = 3 * LANE
GROUP = 8
GROUPS = 5
PARTS = 6
GROUP_OF = (0, 1, 2, 3, 3, 4)
USED = 36
BLOCK = 3 * GROUPS * GROUP
MIB = 1024 * 1024
STEP = 64

sharp = 40.0
rate = 0.5
tiny = 1e-06
guard = 1e-10

f32 = jnp.float32
bf16 = jnp.bfloat16
i32 = jnp.int32


def iota(shape, dim):
    return lax.broadcasted_iota(i32, shape, dim)


def mm(first, second):
    return lax.dot_general(first, second, (((1,), (0,)), ((), ())), preferred_element_type=f32)


def mm_nt(first, second):
    return lax.dot_general(first, second, (((1,), (1,)), ((), ())), preferred_element_type=f32)


def as_half(mask):
    return mask.astype(f32).astype(bf16)


def load(pairs, sems):
    copies = [
        pltpu.make_async_copy(source, target, sems.at[number])
        for number, (source, target) in enumerate(pairs)
    ]
    for copy in copies:
        copy.start()
    return copies


def plan_kernel(src_far, dst_far, neg_far, want_ref, place_ref, src_ref, dst_ref, neg_ref, sems):
    refs = (src_ref, dst_ref, neg_ref)
    loads = load(zip((src_far, dst_far, neg_far), refs), sems)
    for copy in loads:
        copy.wait()
    lists = [refs[kind][step : step + 1, :] for step in range(SUBS) for kind in range(3)]
    holder = iota((HOLD, K), 0)
    hits = [(holder == (row >> 8)).astype(f32) for row in lists]
    upto = as_half(iota((K, K), 0) <= iota((K, K), 1))
    counts = mm(jnp.concatenate(hits, axis=0).astype(bf16), upto)
    want = jnp.zeros((HOLD, LANE), f32)
    slots = iota((LANE, K), 0)
    firsts, lasts = [], []
    for number, row in enumerate(lists):
        step, kind = divmod(number, 3)
        hit = hits[number]
        count = counts[number * HOLD : (number + 1) * HOLD, :]
        order = jnp.sum(hit * count, axis=0, keepdims=True).astype(i32) - 1
        early = order < GROUP
        late = order - GROUP + (4 if kind == 1 else 0)
        slot = jnp.where(early, kind * GROUP + order, GROUP_OF[3 + kind] * GROUP + late)
        owner = row >> 8
        local = (row & 255).astype(f32)
        chosen = as_half(slots == slot + step * STEP)
        want = want + mm_nt((hit * local).astype(bf16), chosen)
        firsts.append(jnp.where(early, owner * GROUP + order, -1))
        lasts.append(jnp.where(early, -1, owner * GROUP + late))
    places = firsts[:3] + lasts[:3] + firsts[3:] + lasts[3:] + [jnp.full((4, K), -1, i32)]
    place_ref[...] = jnp.concatenate(places, axis=0)
    slot = iota((HOLD, LANE), 1) & (STEP - 1)
    want_ref[:, 0, :] = want.astype(i32) + jnp.where(slot < USED, 0, 2 * K)


def part(number):
    return slice(number * K, (number + 1) * K)


def asked(got_ref, step):
    got = got_ref[:, 0, :].astype(f32)
    square = jnp.concatenate([got, jnp.zeros((LANE - HOLD, LANE), f32)], axis=0)
    turned = jnp.transpose(square).astype(i32)
    groups = []
    for group in range(GROUPS):
        start = step * STEP + group * GROUP
        rows = [
            (iota((GROUP, K), 1) == turned[start : start + GROUP, holder : holder + 1]).astype(f32)
            for holder in range(HOLD)
        ]
        groups.append(jnp.concatenate(rows, axis=0))
    half = (iota((K, K), 0) & (GROUP - 1)) < 4
    shared = groups[3]
    return groups[:3] + [jnp.where(half, shared, 0.0), jnp.where(half, 0.0, shared), groups[4]]


def held_kernel(step, got_ref, token_ref, sum_ref):
    del token_ref
    for number, rows in enumerate(asked(got_ref, step)):
        sum_ref[part(number), :] = jnp.transpose(rows).astype(bf16)


def group_mask(shape):
    return (iota(shape, len(shape) - 1) >> 4) == iota(shape, len(shape) - 2)


def pack(values, out_ref):
    keep = group_mask((HOLD, GROUP, LANE))
    sub = iota((HOLD, GROUP, LANE), 1)
    values = [value.reshape(HOLD, GROUP, WIDE) for value in values]
    pieces = [[value[:, :, c * LANE : (c + 1) * LANE] for value in values] for c in range(3)]
    for group, value in enumerate(values):
        row = jnp.sum(jnp.where(keep, value[:, :, REST:], 0.0), axis=1, keepdims=True)
        c, at = divmod(group, 4)
        pieces[c][4] = jnp.where(sub == 4 + at, row, pieces[c][4])
    out_ref[...] = jnp.concatenate(pieces[0] + pieces[1] + pieces[2], axis=1).astype(bf16)


def unpack(in_ref):
    keep = group_mask((HOLD, GROUP, LANE))
    rows = in_ref[...].astype(f32)
    groups = []
    for group in range(GROUPS):
        chunks = []
        for c in range(3):
            start = (c * GROUPS + group) * GROUP
            chunks.append(rows[:, start : start + GROUP, :])
        c, at = divmod(group, 4)
        start = (c * GROUPS + 4) * GROUP + 4 + at
        chunks.append(jnp.where(keep, rows[:, start : start + 1, :], 0.0))
        groups.append(
            jnp.concatenate([x.reshape(K, LANE) for x in chunks], axis=1).astype(bf16)
        )
    return groups


def fold(values):
    tail = values[:, REST:]
    for shift in (64, 32, 16):
        tail = tail + pltpu.roll(tail, shift, 1)
    return tail


def once(tail):
    return jnp.where(iota(tail.shape, 1) < TAIL, tail, 0.0)


def spread_tail(values):
    tail = values[:, REST:]
    for shift in (16, 32, 64):
        tail = tail + pltpu.roll(tail, shift, 1)
    return jnp.concatenate([values[:, :REST], tail], axis=1)


def table_of(values):
    return jnp.concatenate([values[:REST]] + [values[REST:]] * 8, axis=0).astype(bf16)


def table_kernel(left_ref, right_ref, place_ref, got_ref, out_ref, column_ref, signal_ref):
    signal_ref[...] = got_ref[0]
    place = place_ref[...].astype(f32)
    tall = jnp.concatenate([place, jnp.zeros((LANE - 16, K), f32)], axis=0)
    column_ref[...] = jnp.transpose(tall).astype(i32)
    out_ref[:, :K] = table_of(left_ref[...])
    out_ref[:, K:] = table_of(right_ref[...])


def serve(parts, left, right, out_ref):
    tables = (left, right, right, left, right, right)
    values = [mm_nt(rows, table) for rows, table in zip(parts, tables)]
    pack(values[:3] + [values[3] + values[4], values[5]], out_ref)


def serve_kernel(table_ref, got_ref, out_ref, token_ref):
    token_ref[...] = jnp.zeros_like(token_ref)
    parts = [rows.astype(bf16) for rows in asked(got_ref, 0)]
    serve(parts, table_ref[:, :K], table_ref[:, K:], out_ref)


def unit(vectors):
    inverse = 1.0 / jnp.sqrt(jnp.sum(vectors * vectors, axis=-1, keepdims=True) + tiny)
    return vectors * inverse, inverse


def unit_back(grad, direction, inverse):
    return (grad - direction * jnp.sum(direction * grad, axis=-1, keepdims=True)) * inverse


def grad_kernel(step, in_ref, column_ref, place_ref, scale_ref, *refs):
    out_ref = refs[-1]
    rows = unpack(in_ref)

    def picked_part(number):
        at = step * PARTS + number
        to_edge = as_half(iota((K, K), 1) == column_ref[:, at : at + 1])
        return mm(to_edge, rows[GROUP_OF[number]])

    def picked(kind):
        values = picked_part(kind) + picked_part(3 + kind)
        return jnp.concatenate([values[:, :REST], once(fold(values))], axis=1)

    scale = scale_ref[...]
    query, query_inv = unit(picked(0) * scale)
    noise, noise_inv = unit(picked(2))
    query_half = query.astype(bf16)
    noise_half = noise.astype(bf16)
    target, target_inv = unit(picked(1))
    positive = sharp * jnp.sum(query * target, axis=1, keepdims=True)
    scores = sharp * mm_nt(query_half, noise_half)
    raised = jnp.exp(positive)
    spread = jnp.exp(scores)
    total = raised + jnp.sum(spread, axis=1, keepdims=True)
    share = 1.0 / total
    miss = raised * share - 1.0
    weights = spread * share
    query_grad = sharp * (miss * target + mm(weights.astype(bf16), noise_half))
    target_grad = sharp * miss * query
    noise_grad = sharp * mm(jnp.transpose(weights).astype(bf16), query_half)
    grads = [
        unit_back(query_grad, query, query_inv) * scale,
        unit_back(target_grad, target, target_inv),
        unit_back(noise_grad, noise, noise_inv),
    ]
    grads = [spread_tail(grad).astype(bf16) for grad in grads]
    values = []
    for number in range(PARTS):
        at = step * PARTS + number
        to_slot = as_half(iota((K, K), 0) == place_ref[at : at + 1, :])
        values.append(mm(to_slot, grads[number % 3]))
    pack(values[:3] + [values[3] + values[4], values[5]], out_ref)


def adagrad(matrix, state, grad):
    state = state + jnp.sum(grad * grad, axis=0, keepdims=True) / D
    return matrix - grad * (rate / (jnp.sqrt(state) + guard)), state


def row_grads(rows, to_row_ref, numbers):
    values = sum(mm(to_row_ref[part(number), :], rows[GROUP_OF[number]]) for number in numbers)
    values = jnp.concatenate([values[:, :REST], fold(values)], axis=1)
    return jnp.transpose(values)[:D]


LEFT = (0, 3)
RIGHT = (1, 2, 4, 5)


def update(in_ref, to_row_ref, left_ref, right_ref, left_state_ref, right_state_ref):
    rows = unpack(in_ref)
    left = adagrad(left_ref[...], left_state_ref[...], row_grads(rows, to_row_ref, LEFT))
    right = adagrad(right_ref[...], right_state_ref[...], row_grads(rows, to_row_ref, RIGHT))
    return left, right


def next_kernel(
    in_ref, to_row_ref, left_ref, right_ref, left_state_ref, right_state_ref, got_ref,
    out_ref, token_ref,
):
    left, right = update(
        in_ref, to_row_ref, left_ref, right_ref, left_state_ref, right_state_ref
    )
    token_ref[...] = left[0][:8, :LANE]
    parts = [rows.astype(bf16) for rows in asked(got_ref, 1)]
    serve(parts, table_of(left[0]), table_of(right[0]), out_ref)


def update_kernel(
    in_ref, to_row_ref, left_ref, right_ref, left_state_ref, right_state_ref, token_ref,
    left_out, left_state_out, right_out, right_state_out,
):
    del token_ref
    left, right = update(
        in_ref, to_row_ref, left_ref, right_ref, left_state_ref, right_state_ref
    )
    left_out[...], left_state_out[...] = left
    right_out[...], right_state_out[...] = right


def right_last_kernel(in_ref, to_row_ref, right_ref, right_state_ref, joined_ref):
    grads = row_grads(unpack(in_ref), to_row_ref, RIGHT)
    right, state = adagrad(right_ref[...], right_state_ref[...], grads)
    joined_ref[...] = jnp.concatenate([right, jnp.broadcast_to(state, (8, K))], axis=0)


def left_last_kernel(in_ref, to_row_ref, left_ref, left_state_ref, left_out, left_state_out):
    grads = row_grads(unpack(in_ref), to_row_ref, LEFT)
    left_out[...], left_state_out[...] = adagrad(left_ref[...], left_state_ref[...], grads)


def call(kernel, outs, *args, far=(), scratch=(), copies=0, grant=16):
    size = sum(x.size * x.dtype.itemsize for x in list(args) + list(outs))
    held = pl.BlockSpec(memory_space=pltpu.VMEM)
    away = pl.BlockSpec(memory_space=pltpu.HBM)
    scratch = [pltpu.VMEM(x.shape, x.dtype) for x in scratch]
    if copies:
        scratch.append(pltpu.SemaphoreType.DMA((copies,)))
    return pl.pallas_call(
        kernel,
        out_shape=tuple(outs),
        in_specs=[away if number in far else held for number in range(len(args))],
        out_specs=tuple([held] * len(outs)),
        scratch_shapes=scratch,
        compiler_params=pltpu.CompilerParams(vmem_limit_bytes=grant * MIB),
        cost_estimate=pl.CostEstimate(flops=0, bytes_accessed=size, transcendentals=0),
    )(*args)


def shape(dims, dtype):
    return jax.ShapeDtypeStruct(dims, dtype)


def exchange(blocks):
    return lax.all_to_all(blocks, "edge", split_axis=0, concat_axis=0, tiled=True)


def shifted(value, axis, steps):
    count = lax.axis_size(axis)
    pairs = [(source, (source + steps) % count) for source in range(count)]
    return lax.ppermute(value, axis, pairs)


BLOCKS = shape((HOLD, BLOCK, LANE), bf16)
TABLE = shape((D, K), f32)
STATE = shape((1, K), f32)
LIST = shape((SUBS, K), i32)
HOT = shape((PARTS * K, K), bf16)
TOKEN = shape((8, LANE), f32)


def holds_of(step, got, token):
    return call(functools.partial(held_kernel, step), [HOT], got, token)[0]


def grads_of(step, blocks, columns, place, scales, *tokens):
    return call(
        functools.partial(grad_kernel, step), [BLOCKS],
        blocks, columns, place, scales[step * K : (step + 1) * K], *tokens,
    )[0]


def on_device(
    left_emb, right_emb, left_state, right_state, relations, src_rows, dst_rows, rel_ids, neg_rows
):
    left, right = left_emb.T, right_emb.T
    left_hist, right_hist = left_state.reshape(1, K), right_state.reshape(1, K)
    want, place = call(
        plan_kernel, [shape((HOLD, 1, LANE), i32), shape((16, K), i32)],
        src_rows[0], dst_rows[0], neg_rows[0],
        far=(0, 1, 2), scratch=(LIST, LIST, LIST), copies=3, grant=62,
    )
    even = lax.axis_index("bucket") % 2 == 0
    first = lax.cond(even, exchange, jnp.zeros_like, want)
    table, columns, signal = call(
        table_kernel,
        [shape((WIDE, 2 * K), bf16), shape((K, LANE), i32), shape((1, LANE), i32)],
        left, right, place, first,
    )
    pairs = [(bucket, bucket + 1) for bucket in range(0, lax.axis_size("bucket") - 1, 2)]
    signal = lax.ppermute(signal, "bucket", pairs)
    want = jnp.where(signal[0, 0] < 0, 0, want)
    got = lax.cond(even, lambda one, two: one, lambda one, two: exchange(two), first, want)
    scales = jnp.pad(relations[rel_ids[0].reshape(-1)], ((0, 0), (0, WIDE - D)))
    blocks, token = call(serve_kernel, [BLOCKS, TOKEN], table, got)
    blocks = exchange(blocks)
    to_row = holds_of(0, got, token)
    blocks = grads_of(0, blocks, columns, place, scales, to_row)
    blocks = exchange(blocks)
    held = (blocks, to_row, left, right, left_hist, right_hist)
    blocks, token = call(next_kernel, [BLOCKS, TOKEN], *held, got)
    blocks = exchange(blocks)
    left, left_hist, right, right_hist = call(
        update_kernel, [TABLE, STATE, TABLE, STATE], *held, token
    )
    to_row = holds_of(1, got, left_hist)
    blocks = grads_of(1, blocks, columns, place, scales, to_row)
    blocks = exchange(blocks)
    (joined,) = call(
        right_last_kernel, [shape((D + 8, K), f32)], blocks, to_row, right, right_hist
    )
    joined = shifted(joined, "bucket", 1)
    left, left_hist = call(left_last_kernel, [TABLE, STATE], blocks, to_row, left, left_hist)
    return (left.T, left_hist.reshape(K), joined[:D].T, joined[D])


def solution(mesh):
    return jax.shard_map(
        on_device,
        mesh=mesh,
        in_specs=(
            P(("bucket", "edge"), None),
            P(("bucket", "edge"), None),
            P(("bucket", "edge")),
            P(("bucket", "edge")),
            P(),
            P("bucket", None, "edge"),
            P("bucket", None, "edge"),
            P("bucket", None, "edge"),
            P("bucket", None, "edge"),
        ),
        out_specs=(
            P(("bucket", "edge"), None),
            P(("bucket", "edge")),
            P(("bucket", "edge"), None),
            P(("bucket", "edge")),
        ),
        check_vma=False,
    )
```
